512 devices in a mesh: dp: 64 (over y, z), col: 8 (over x, core).
Axes of the slice: x: 4, y: 4, z: 16, core: 2. Of those that a mesh axis runs over, the one named last changes fastest.
Arguments:
- tokens: bfloat16 [16384, 8192], P('dp', 'col'), may hold values from -6 to 6
- basis: bfloat16 [8192, 256], P('dp'), may hold values from -0.0625 to 0.0625
- grad_out: bfloat16 [16384, 28672], P('dp', 'col'), may hold values from -0.046875 to 0.046875
- first_moment: float32 [256, 28672], P('dp', 'col'), may hold values from -3 to 3
- second_moment: float32 [256, 28672], P('dp', 'col'), may hold values from 0.002 to 0.02
Outputs:
- new_first: float32 [256, 28672], P('dp', 'col')
- new_second: float32 [256, 28672], P('dp', 'col')
- update: float32 [8192, 28672], P('dp', 'col')
The draws below stay inside these ranges and needn't reach their ends.
All inputs are finite; a program needn't handle non-finite values.
Results may differ from the reference program's by a relative error of at most 0.003.
Values may be sent and summed in bfloat16 or wider, within the bound.
No kernel may reach another device: no remote copies, remote signals or barrier semaphores. Data moves between devices by JAX's collectives and lax.ppermute only.
A program may use at most 64 MiB of HBM per device.

```python
import math
import jax
import jax.numpy as jnp

D = 8192
F = 28672
R = 256
STEP = 10
TOKENS = 16384


def level_of(stream_key, shape, shards, least, largest):
    def one(dim, blocks):
        steps = jax.random.uniform(jax.random.fold_in(jax.random.fold_in(stream_key, 6), dim), (blocks,), jnp.float32, least / len(shards), largest / len(shards))
        return jnp.repeat(jnp.exp(steps), shape[dim] // blocks).reshape((-1,) + (1,) * (len(shape) - dim - 1))

    loudness = one(*shards[0])
    for cut in shards[1:]:
        loudness = loudness * one(*cut)
    return loudness


def gaussian(key, shape, spread, limit, shards=(), dtype=jnp.bfloat16):
    level = level_of(key, shape, shards, -0.22, 0.18) if shards else 1.0
    values = jax.random.normal(key, shape, jnp.float32) * spread * level
    return jnp.minimum(jnp.maximum(values, -limit), limit).astype(dtype)


def setup_inputs(seed: int = 0) -> dict:
    seeds = jax.random.split(jax.random.key(seed), 6)
    tokens = gaussian(seeds[0], (TOKENS, D), 1.0, 6.0, ((0, 64), (1, 8)))
    basis = gaussian(seeds[1], (D, R), D ** -0.5, 0.0625, ((0, 64),))
    grad_out = gaussian(seeds[2], (TOKENS, F), (TOKENS ** -0.5), 0.046875, ((0, 64), (1, 8)))
    first_moment = gaussian(seeds[3], (R, F), 0.5, 3.0, ((0, 64), (1, 8)), jnp.float32)
    second_moment = jnp.clip(jnp.exp(math.log(0.02) - 2.30258502 * jax.random.uniform(seeds[4], (R, F), jnp.float32) ** level_of(seeds[4], (R, F), ((0, 64), (1, 8)), -0.2, 0.2)), 0.002, 0.02)
    return dict(tokens=tokens, basis=basis, grad_out=grad_out, first_moment=first_moment, second_moment=second_moment)


def reference(tokens, basis, grad_out, first_moment, second_moment):
    projected = jnp.dot(tokens, basis, preferred_element_type=jnp.float32).astype(jnp.bfloat16)
    gradient = jnp.dot(projected.T, grad_out, preferred_element_type=jnp.float32)
    new_first = 0.9 * first_moment + 0.1 * gradient
    new_second = 0.999 * second_moment + 0.001 * gradient * gradient
    first_scale = 1.0 - 0.9 ** STEP
    second_scale = 1.0 - 0.999 ** STEP
    direction = new_first / first_scale / (jnp.sqrt(new_second / second_scale) + 1e-08)
    direction = direction.astype(jnp.bfloat16)
    update = jnp.dot(basis, direction, preferred_element_type=jnp.float32)
    return (new_first, new_second, update)
```

```python
import jax
import jax.numpy as jnp
from jax import lax
from jax.sharding import Mesh, PartitionSpec as P

STEP = 10
Y, Z, X, C = 4, 16, 4, 2
bf16, f32 = jnp.bfloat16, jnp.float32


def exchange(x, axes):
    return lax.all_to_all(x, axes, 0, 0, tiled=True)


def gather(x, axes, n):
    return exchange(jnp.broadcast_to(x[None], (n,) + x.shape), axes)


def rank_order(first, count, ranks):
    share = ranks // (Y * Z)
    place = lax.broadcasted_iota(jnp.int32, (ranks, count), 1) + first
    z, y, j = place // (Y * share), place // share % Y, place % share
    rank = (y * Z + z) * share + j
    return (lax.broadcasted_iota(jnp.int32, (ranks, count), 0) == rank).astype(bf16)


def adam(first_moment, second_moment, gradient):
    new_first = 0.9 * first_moment + 0.1 * gradient
    new_second = 0.999 * second_moment + 0.001 * gradient * gradient
    return new_first, new_second


def on_device(tokens, basis, grad_out, first_moment, second_moment):
    rows, ranks = basis.shape
    count, features = tokens.shape
    share, columns = first_moment.shape
    part = columns // Y
    half = ranks // C
    core = lax.axis_index("c")

    ordered_half = jnp.dot(basis, rank_order(core * half, half, ranks), preferred_element_type=f32).astype(bf16)
    turned = lax.ppermute(ordered_half, ("y", "x"), [(y * X + x, x * X + y) for y in range(Y) for x in range(X)])
    chip_basis = gather(turned, "z", Z).reshape(C, features, half)

    other = lax.ppermute(tokens, "c", [(0, 1), (1, 0)])

    cut = grad_out.reshape(count, Y, part).transpose(1, 0, 2)
    all_grad_out = exchange(cut, "y").reshape(Y * count, part)

    ordered = jnp.dot(basis, rank_order(0, ranks, ranks), preferred_element_type=f32).astype(bf16)
    y_basis = gather(ordered, "y", Y).reshape(Y * rows, ranks)
    moments = jnp.concatenate([first_moment, second_moment], 0).reshape(2 * share, Y, part).transpose(1, 0, 2)
    moments = exchange(moments, "y").reshape(Y, 2, share, part)
    first_part = moments[:, 0].reshape(Y * share, part)
    second_part = moments[:, 1].reshape(Y * share, part)

    mine = lax.dynamic_index_in_dim(chip_basis, core, 0, keepdims=False)
    theirs = lax.dynamic_index_in_dim(chip_basis, 1 - core, 0, keepdims=False)
    summed = jnp.dot(tokens, mine, preferred_element_type=f32) + jnp.dot(other, theirs, preferred_element_type=f32)
    summed = exchange(summed.reshape(X, count // X, half), "x").sum(0)
    projected = gather(summed.astype(bf16), ("c", "y", "x"), C * Y * X).reshape(C, Y * count, half)

    partial = jnp.concatenate(
        [
            lax.dot_general(projected[c], all_grad_out, (((0,), (0,)), ((), ())), preferred_element_type=f32)
            for c in range(C)
        ],
        0,
    )
    partial = partial.astype(bf16).reshape(Z, Y * share, part)
    gradient = exchange(partial, "z").astype(f32).sum(0)

    first_scale = 1.0 - 0.9**STEP
    second_scale = 1.0 - 0.999**STEP
    new_first, new_second = adam(first_part, second_part, gradient)
    direction = new_first / first_scale / (jnp.sqrt(new_second / second_scale) + 1e-08)
    all_direction = gather(direction.astype(bf16), "z", Z).reshape(ranks, part)
    update = jnp.dot(y_basis, all_direction, preferred_element_type=f32).astype(bf16)
    update = exchange(update.reshape(Y, rows, part), "y").transpose(1, 0, 2).reshape(rows, columns).astype(f32)

    own = exchange(gradient.reshape(Y, share, part), "y").transpose(1, 0, 2).reshape(share, columns)
    new_first, new_second = adam(first_moment, second_moment, own)
    return (new_first, new_second, update)


def solution(mesh):
    grid = Mesh(mesh.devices.reshape(Y, Z, X, C), ("y", "z", "x", "c"))
    dp, col = ("y", "z"), ("x", "c")
    return jax.shard_map(
        on_device,
        mesh=grid,
        in_specs=(P(dp, col), P(dp, None), P(dp, col), P(dp, col), P(dp, col)),
        out_specs=(P(dp, col), P(dp, col), P(dp, col)),
        check_vma=False,
    )
```

```python
import jax
import jax.numpy as jnp
from jax import lax
from jax.experimental import pallas as pl
from jax.experimental.pallas import tpu as pltpu
from jax.sharding import Mesh, PartitionSpec as P

STEP = 10
Y, Z, X, C = 4, 16, 4, 2
bf16, f32 = jnp.bfloat16, jnp.float32
VMEM = pl.BlockSpec(memory_space=pltpu.VMEM)


def exchange(x, axes):
    return lax.all_to_all(x, axes, 0, 0, tiled=True)


def gather(x, axes, n):
    return exchange(jnp.broadcast_to(x[None], (n,) + x.shape), axes)


def send(x, step):
    return lax.ppermute(x, "y", [(y, (y + step) % Y) for y in range(Y)])


def in_order(parts, me):
    twice = jnp.stack(parts[::-1] * 2)
    return lax.dynamic_slice_in_dim(twice, (Y - 1 - me) % Y, Y, 0)


def rank_order(first, count, ranks):
    share = ranks // (Y * Z)
    place = lax.broadcasted_iota(jnp.int32, (ranks, count), 1) + first
    z, y, j = place // (Y * share), place // share % Y, place % share
    rank = (y * Z + z) * share + j
    return (lax.broadcasted_iota(jnp.int32, (ranks, count), 0) == rank).astype(bf16)


def adam(first_moment, second_moment, gradient):
    new_first = 0.9 * first_moment + 0.1 * gradient
    new_second = 0.999 * second_moment + 0.001 * gradient * gradient
    return new_first, new_second


def partial_kernel(me_ref, joined_ref, *refs):
    grads, out_ref = refs[:Y], refs[Y]
    count = grads[0].shape[0]
    half = joined_ref.shape[3]
    for c in range(C):
        total = 0.0
        for d in range(Y):
            source = lax.rem(me_ref[0] + Y - d, Y)
            tokens = joined_ref[c, source, :count, :]
            total += lax.dot_general(tokens, grads[d][...], (((0,), (0,)), ((), ())), preferred_element_type=f32)
        out_ref[c * half : (c + 1) * half, :] = total.astype(bf16)


def adam_kernel(pieces_ref, first_ref, second_ref, gradient_ref, direction_ref):
    gradient = jnp.sum(pieces_ref[...].astype(f32), axis=0)
    gradient_ref[...] = gradient
    first_scale = 1.0 - 0.9**STEP
    second_scale = 1.0 - 0.999**STEP
    new_first, new_second = adam(first_ref[...], second_ref[...], gradient)
    direction = new_first / first_scale / (jnp.sqrt(new_second / second_scale) + 1e-08)
    direction_ref[...] = jnp.broadcast_to(direction.astype(bf16)[None], direction_ref.shape)


def update_kernel(joined_ref, direction_ref, out_ref):
    rows = out_ref.shape[1]
    half = joined_ref.shape[3]
    for y in range(Y):
        total = 0.0
        for c in range(C):
            basis = joined_ref[c, y, joined_ref.shape[2] - rows :, :]
            total += jnp.dot(basis, direction_ref[c * half : (c + 1) * half, :], preferred_element_type=f32)
        out_ref[y] = total.astype(bf16)


def on_device(tokens, basis, grad_out, first_moment, second_moment):
    rows, ranks = basis.shape
    count, features = tokens.shape
    share, columns = first_moment.shape
    part = columns // Y
    half = ranks // C
    core = lax.axis_index("c")
    me = lax.axis_index("y")

    ordered_half = jnp.dot(basis, rank_order(core * half, half, ranks), preferred_element_type=f32).astype(bf16)
    turned = lax.ppermute(ordered_half, ("y", "x"), [(y * X + x, x * X + y) for y in range(Y) for x in range(X)])
    chip_basis = gather(turned, "z", Z).reshape(C, features, half)

    other = lax.ppermute(tokens, "c", [(0, 1), (1, 0)])

    def columns_of(x, step):
        return lax.dynamic_slice_in_dim(x, (me + step) % Y * part, part, 1)

    grads = [columns_of(grad_out, 0)] + [send(columns_of(grad_out, d), d) for d in range(1, Y)]

    moments = jnp.concatenate([first_moment, second_moment], 0)
    moments = [columns_of(moments, 0)] + [send(columns_of(moments, d), d) for d in range(1, Y)]

    mine = lax.dynamic_index_in_dim(chip_basis, core, 0, keepdims=False)
    theirs = lax.dynamic_index_in_dim(chip_basis, 1 - core, 0, keepdims=False)
    summed = jnp.dot(tokens, mine, preferred_element_type=f32) + jnp.dot(other, theirs, preferred_element_type=f32)
    summed = gather(summed, "x", X).sum(0)
    summed, grads, moments = lax.optimization_barrier((summed, grads, moments))
    moments = in_order(moments, me)
    first_part = moments[:, :share].reshape(Y * share, part)
    second_part = moments[:, share:].reshape(Y * share, part)

    joined = jnp.concatenate([summed.astype(bf16), ordered_half], 0)
    joined = gather(joined, ("c", "y"), C * Y).reshape(C, Y, count + rows, half)

    partial = pl.pallas_call(
        partial_kernel,
        out_shape=jax.ShapeDtypeStruct((ranks, part), bf16),
        in_specs=[pl.BlockSpec(memory_space=pltpu.SMEM)] + [VMEM] * (1 + Y),
        out_specs=VMEM,
        compiler_params=pltpu.CompilerParams(vmem_limit_bytes=24 * 2**20),
        name="gradient_partial",
    )(me.reshape(1), joined, *grads)
    pieces = exchange(partial.reshape(Z, Y * share, part), "z")
    gradient, direction = pl.pallas_call(
        adam_kernel,
        out_shape=(
            jax.ShapeDtypeStruct((Y * share, part), f32),
            jax.ShapeDtypeStruct((Z, Y * share, part), bf16),
        ),
        in_specs=[VMEM] * 3,
        out_specs=(VMEM, VMEM),
        compiler_params=pltpu.CompilerParams(vmem_limit_bytes=24 * 2**20),
        name="sum_and_adam",
    )(pieces, first_part, second_part)
    all_direction = exchange(direction, "z").reshape(ranks, part)
    update = pl.pallas_call(
        update_kernel,
        out_shape=jax.ShapeDtypeStruct((Y, rows, part), bf16),
        in_specs=[VMEM] * 2,
        out_specs=VMEM,
        compiler_params=pltpu.CompilerParams(vmem_limit_bytes=24 * 2**20),
        name="update",
    )(joined, all_direction)
    update = exchange(update, "y").transpose(1, 0, 2).reshape(rows, columns).astype(f32)

    def rows_of(x, step):
        return lax.dynamic_slice_in_dim(x, (me + step) % Y * share, share, 0)

    own = in_order([rows_of(gradient, 0)] + [send(rows_of(gradient, d), d) for d in range(1, Y)], me)
    own = own.transpose(1, 0, 2).reshape(share, columns)
    new_first, new_second = adam(first_moment, second_moment, own)
    return (new_first, new_second, update)


def solution(mesh):
    grid = Mesh(mesh.devices.reshape(Y, Z, X, C), ("y", "z", "x", "c"))
    dp, col = ("y", "z"), ("x", "c")
    return jax.shard_map(
        on_device,
        mesh=grid,
        in_specs=(P(dp, col), P(dp, None), P(dp, col), P(dp, col), P(dp, col)),
        out_specs=(P(dp, col), P(dp, col), P(dp, col)),
        check_vma=False,
    )
```

```python
import jax
import jax.numpy as jnp
from jax import lax
from jax.experimental import pallas as pl
from jax.experimental.pallas import tpu as pltpu
from jax.sharding import Mesh, PartitionSpec as P

STEP = 10
Y, Z, X, C = 4, 16, 4, 2
PACK = 48
MOMENT_ROWS = 32
bf16, f32 = jnp.bfloat16, jnp.float32
VMEM = pl.BlockSpec(memory_space=pltpu.VMEM)
SMEM = pl.BlockSpec(memory_space=pltpu.SMEM)


def exchange(x, axes):
    return lax.all_to_all(x, axes, 0, 0, tiled=True)


def gather(x, axes, n):
    return exchange(jnp.broadcast_to(x[None], (n,) + x.shape), axes)


def send(x, step):
    return lax.ppermute(x, "y", [(y, (y + step) % Y) for y in range(Y)])


def call(kernel, name, out, *args):
    return pl.pallas_call(
        kernel,
        out_shape=[jax.ShapeDtypeStruct(shape, dtype) for shape, dtype in out],
        in_specs=[SMEM] + [VMEM] * (len(args) - 1),
        out_specs=[VMEM] * len(out),
        compiler_params=pltpu.CompilerParams(vmem_limit_bytes=32 * 2**20),
        name=name,
    )(*args)


def rank_order(first, count, ranks):
    share = ranks // (Y * Z)
    place = lax.broadcasted_iota(jnp.int32, (ranks, count), 1) + first
    z, y, j = place // (Y * share), place // share % Y, place % share
    rank = (y * Z + z) * share + j
    return (lax.broadcasted_iota(jnp.int32, (ranks, count), 0) == rank).astype(bf16)


def three_parts(x):
    high = x.astype(bf16).astype(f32)
    rest = x - high
    middle = rest.astype(bf16).astype(f32)
    return high, middle, rest - middle


def adam(first_moment, second_moment, gradient):
    new_first = 0.9 * first_moment + 0.1 * gradient
    new_second = 0.999 * second_moment + 0.001 * gradient * gradient
    return new_first, new_second


def source(me, d):
    return (me + Y - d) & (Y - 1)


def pack_kernel(at_ref, basis_ref, grad_ref, moments_ref, *outs):
    part = outs[0].shape[1]
    count = grad_ref.shape[0]
    rows, ranks = basis_ref.shape
    for d in range(Y):
        begin = pl.multiple_of(((at_ref[0] + d) & (Y - 1)) * part, 128)
        outs[d][:count, :] = grad_ref[:, pl.ds(begin, part)]
        for k in range(3):
            take = min(PACK, rows - k * PACK)
            outs[d][count : count + take, k * ranks : (k + 1) * ranks] = basis_ref[k * PACK : k * PACK + take, :]
        parts = three_parts(moments_ref[:, pl.ds(begin, part)])
        parts = jnp.concatenate(parts + (jnp.zeros_like(parts[0]),), 0)
        outs[d][count + PACK :, :] = parts.astype(bf16)


def project_kernel(at_ref, tokens_ref, other_ref, basis_ref, out_ref):
    core = at_ref[1]
    total = jnp.dot(tokens_ref[...], basis_ref[core], preferred_element_type=f32)
    total += jnp.dot(other_ref[...], basis_ref[1 - core], preferred_element_type=f32)
    for x in range(out_ref.shape[0]):
        out_ref[x] = total


def round_kernel(at_ref, summands_ref, out_ref):
    total = jnp.sum(summands_ref[...], axis=0).astype(bf16)
    for i in range(out_ref.shape[0]):
        out_ref[i] = total


def partial_kernel(at_ref, projected_ref, *refs):
    messages, out_ref = refs[:Y], refs[Y]
    count, half = projected_ref.shape[2:]
    for c in range(C):
        total = 0.0
        for d in range(Y):
            tokens = projected_ref[c, source(at_ref[0], d)]
            total += lax.dot_general(tokens, messages[d][:count, :], (((0,), (0,)), ((), ())), preferred_element_type=f32)
        out_ref[c * half : (c + 1) * half, :] = total.astype(bf16)


def moments_kernel(at_ref, *refs):
    messages, (first_ref, second_ref) = refs[:Y], refs[Y:]
    ranks = first_ref.shape[0]
    stack = jnp.concatenate([m[m.shape[0] - MOMENT_ROWS :, :] for m in messages], 0)
    shape = (6 * ranks, stack.shape[0])
    row, column = lax.broadcasted_iota(jnp.int32, shape, 0), lax.broadcasted_iota(jnp.int32, shape, 1)
    which, rank = row // ranks, row % ranks
    moment, piece = which // 3, which % 3
    block = (at_ref[0] + Y - rank // 4) & (Y - 1)
    pick = (column == block * MOMENT_ROWS + piece * 8 + moment * 4 + rank % 4).astype(bf16)
    picked = jnp.dot(pick, stack, preferred_element_type=f32)
    for m, out_ref in enumerate((first_ref, second_ref)):
        high, middle, low = (picked[(3 * m + p) * ranks : (3 * m + p + 1) * ranks, :] for p in range(3))
        out_ref[...] = high + middle + low


def adam_kernel(at_ref, pieces_ref, first_ref, second_ref, gradient_ref, direction_ref):
    gradient = jnp.sum(pieces_ref[...].astype(f32), axis=0)
    gradient_ref[...] = gradient
    first_scale = 1.0 - 0.9**STEP
    second_scale = 1.0 - 0.999**STEP
    new_first, new_second = adam(first_ref[...], second_ref[...], gradient)
    direction = new_first / first_scale / (jnp.sqrt(new_second / second_scale) + 1e-08)
    direction = direction.astype(bf16)
    for h in range(direction_ref.shape[0]):
        direction_ref[h] = direction


def update_kernel(at_ref, direction_ref, gradient_ref, *refs):
    messages, out_ref = refs[:Y], refs[Y]
    count = messages[0].shape[0] - PACK - MOMENT_ROWS
    ranks = direction_ref.shape[0]
    rows = out_ref.shape[1] - 16
    direction = direction_ref[...]
    for d in range(Y):
        pieces = []
        for k in range(3):
            take = min(PACK, rows - k * PACK)
            pieces.append(messages[d][count : count + take, k * ranks : (k + 1) * ranks])
        basis = jnp.concatenate(pieces, 0)
        out_ref[source(at_ref[0], d), :rows, :] = jnp.dot(basis, direction, preferred_element_type=f32).astype(bf16)
    parts = jnp.concatenate(three_parts(gradient_ref[...]), 0).astype(bf16)
    shape = (Y * 16, parts.shape[0])
    row, column = lax.broadcasted_iota(jnp.int32, shape, 0), lax.broadcasted_iota(jnp.int32, shape, 1)
    place = row % 16
    wanted = place // 4 * gradient_ref.shape[0] + row // 16 * 4 + place % 4
    pick = ((column == wanted) & (place < 12)).astype(bf16)
    picked = jnp.dot(pick, parts, preferred_element_type=f32).astype(bf16)
    for y in range(Y):
        out_ref[y, rows:, :] = picked[16 * y : 16 * (y + 1), :]


def finish_kernel(at_ref, arrived_ref, first_ref, second_ref, new_first_ref, new_second_ref, update_ref):
    rows = update_ref.shape[0]
    part = arrived_ref.shape[2]
    for y in range(Y):
        columns = slice(y * part, (y + 1) * part)
        update_ref[:, columns] = arrived_ref[y, :rows, :].astype(f32)
        parts = arrived_ref[y, rows:, :].astype(f32)
        gradient = parts[0:4] + parts[4:8] + parts[8:12]
        new_first, new_second = adam(first_ref[:, columns], second_ref[:, columns], gradient)
        new_first_ref[:, columns] = new_first
        new_second_ref[:, columns] = new_second


def on_device(tokens, basis, grad_out, first_moment, second_moment):
    rows, ranks = basis.shape
    count, features = tokens.shape
    share, columns = first_moment.shape
    part = columns // Y
    half = ranks // C
    core = lax.axis_index("c")
    at = jnp.stack([lax.axis_index("y"), core])

    ordered_half = jnp.dot(basis, rank_order(core * half, half, ranks), preferred_element_type=f32).astype(bf16)
    turned = lax.ppermute(ordered_half, ("y", "x"), [(y * X + x, x * X + y) for y in range(Y) for x in range(X)])
    chip_basis = gather(turned, "z", Z).reshape(C, features, half)

    other = lax.ppermute(tokens, "c", [(0, 1), (1, 0)])

    ordered = jnp.dot(basis, rank_order(0, ranks, ranks), preferred_element_type=f32).astype(bf16)
    moments = jnp.concatenate([first_moment, second_moment], 0)
    message = (count + PACK + MOMENT_ROWS, part)
    messages = call(pack_kernel, "pack", [(message, bf16)] * Y, at, ordered, grad_out, moments)
    messages = [messages[0]] + [send(messages[d], d) for d in range(1, Y)]

    (summands,) = call(project_kernel, "project", [((X, count, half), f32)], at, tokens, other, chip_basis)
    summands = exchange(summands, "x")
    (projected,) = call(round_kernel, "round", [((C * Y, count, half), bf16)], at, summands)
    projected, messages = lax.optimization_barrier((projected, messages))
    projected = exchange(projected, ("c", "y")).reshape(C, Y, count, half)

    (partial,) = call(partial_kernel, "partial", [((ranks, part), bf16)], at, projected, *messages)
    pieces = exchange(partial.reshape(Z, ranks // Z, part), "z")
    first, second = call(moments_kernel, "moments", [((ranks // Z, part), f32)] * 2, at, *messages)
    gradient, direction = call(
        adam_kernel,
        "sum_and_adam",
        [((ranks // Z, part), f32), ((Z, ranks // Z, part), bf16)],
        at,
        pieces,
        first,
        second,
    )
    direction = exchange(direction, "z").reshape(ranks, part)
    (update,) = call(update_kernel, "update", [((Y, rows + 16, part), bf16)], at, direction, gradient, *messages)
    arrived = exchange(update, "y")
    return tuple(
        call(
            finish_kernel,
            "finish",
            [((share, columns), f32), ((share, columns), f32), ((rows, columns), f32)],
            at,
            arrived,
            first_moment,
            second_moment,
        )
    )


def solution(mesh):
    grid = Mesh(mesh.devices.reshape(Y, Z, X, C), ("y", "z", "x", "c"))
    dp, col = ("y", "z"), ("x", "c")
    return jax.shard_map(
        on_device,
        mesh=grid,
        in_specs=(P(dp, col), P(dp, None), P(dp, col), P(dp, col), P(dp, col)),
        out_specs=(P(dp, col), P(dp, col), P(dp, col)),
        check_vma=False,
    )
```

```python
import jax
import jax.numpy as jnp
from jax import lax
from jax.experimental import pallas as pl
from jax.experimental.pallas import tpu as pltpu
from jax.sharding import Mesh, PartitionSpec as P

STEP = 10
Y, Z, X, C = 4, 16, 4, 2
PACK = 48
MOMENT_ROWS = 32
bf16, f32 = jnp.bfloat16, jnp.float32
VMEM = pl.BlockSpec(memory_space=pltpu.VMEM)
SMEM = pl.BlockSpec(memory_space=pltpu.SMEM)


def exchange(x, axes):
    return lax.all_to_all(x, axes, 0, 0, tiled=True)


def gather(x, axes, n):
    return exchange(jnp.broadcast_to(x[None], (n,) + x.shape), axes)


def send(x, step):
    return lax.ppermute(x, "y", [(y, (y + step) % Y) for y in range(Y)])


def call(kernel, name, out, *args):
    return pl.pallas_call(
        kernel,
        out_shape=[jax.ShapeDtypeStruct(shape, dtype) for shape, dtype in out],
        in_specs=[SMEM] + [VMEM] * (len(args) - 1),
        out_specs=[VMEM] * len(out),
        compiler_params=pltpu.CompilerParams(vmem_limit_bytes=32 * 2**20),
        name=name,
    )(*args)


def rank_order(first, count, ranks):
    share = ranks // (Y * Z)
    place = lax.broadcasted_iota(jnp.int32, (ranks, count), 1) + first
    z, y, j = place // (Y * share), place // share % Y, place % share
    rank = (y * Z + z) * share + j
    return (lax.broadcasted_iota(jnp.int32, (ranks, count), 0) == rank).astype(bf16)


def three_parts(x):
    high = x.astype(bf16).astype(f32)
    rest = x - high
    middle = rest.astype(bf16).astype(f32)
    return high, middle, rest - middle


def adam(first_moment, second_moment, gradient):
    new_first = 0.9 * first_moment + 0.1 * gradient
    new_second = 0.999 * second_moment + 0.001 * gradient * gradient
    return new_first, new_second


def source(me, d):
    return (me + Y - d) & (Y - 1)


def pack_kernel(at_ref, basis_ref, grad_ref, moments_ref, *outs):
    part = outs[0].shape[1]
    count = grad_ref.shape[0]
    rows, ranks = basis_ref.shape
    for d in range(Y):
        begin = pl.multiple_of(((at_ref[0] + d) & (Y - 1)) * part, 128)
        outs[d][:count, :] = grad_ref[:, pl.ds(begin, part)]
        for k in range(3):
            take = min(PACK, rows - k * PACK)
            outs[d][count : count + take, k * ranks : (k + 1) * ranks] = basis_ref[k * PACK : k * PACK + take, :]
        parts = three_parts(moments_ref[:, pl.ds(begin, part)])
        parts = jnp.concatenate(parts + (jnp.zeros_like(parts[0]),), 0)
        outs[d][count + PACK :, :] = parts.astype(bf16)


def project_kernel(at_ref, tokens_ref, other_ref, basis_ref, out_ref):
    core = at_ref[1]
    total = jnp.dot(tokens_ref[...], basis_ref[core], preferred_element_type=f32)
    total += jnp.dot(other_ref[...], basis_ref[1 - core], preferred_element_type=f32)
    for x in range(out_ref.shape[0]):
        out_ref[x] = total


def round_kernel(at_ref, summands_ref, out_ref):
    total = jnp.sum(summands_ref[...], axis=0).astype(bf16)
    for i in range(out_ref.shape[0]):
        out_ref[i] = total


def partial_kernel(at_ref, projected_ref, *refs):
    messages, out_ref = refs[:Y], refs[Y]
    count, half = projected_ref.shape[2:]
    for c in range(C):
        total = 0.0
        for d in range(Y):
            tokens = projected_ref[c, source(at_ref[0], d)]
            total += lax.dot_general(tokens, messages[d][:count, :], (((0,), (0,)), ((), ())), preferred_element_type=f32)
        out_ref[c * half : (c + 1) * half, :] = total.astype(bf16)


def moments_kernel(at_ref, *refs):
    messages, (first_ref, second_ref) = refs[:Y], refs[Y:]
    ranks = first_ref.shape[0]
    stack = jnp.concatenate([m[m.shape[0] - MOMENT_ROWS :, :] for m in messages], 0)
    shape = (6 * ranks, stack.shape[0])
    row, column = lax.broadcasted_iota(jnp.int32, shape, 0), lax.broadcasted_iota(jnp.int32, shape, 1)
    which, rank = row // ranks, row % ranks
    moment, piece = which // 3, which % 3
    block = (at_ref[0] + Y - rank // 4) & (Y - 1)
    pick = (column == block * MOMENT_ROWS + piece * 8 + moment * 4 + rank % 4).astype(bf16)
    picked = jnp.dot(pick, stack, preferred_element_type=f32)
    for m, out_ref in enumerate((first_ref, second_ref)):
        high, middle, low = (picked[(3 * m + p) * ranks : (3 * m + p + 1) * ranks, :] for p in range(3))
        out_ref[...] = high + middle + low


def adam_kernel(at_ref, pieces_ref, first_ref, second_ref, gradient_ref, direction_ref):
    gradient = jnp.sum(pieces_ref[...].astype(f32), axis=0)
    gradient_ref[...] = gradient
    first_scale = 1.0 - 0.9**STEP
    second_scale = 1.0 - 0.999**STEP
    new_first, new_second = adam(first_ref[...], second_ref[...], gradient)
    direction = new_first / first_scale / (jnp.sqrt(new_second / second_scale) + 1e-08)
    direction = direction.astype(bf16)
    for h in range(direction_ref.shape[0]):
        direction_ref[h] = direction


def update_kernel(at_ref, direction_ref, gradient_ref, *refs):
    messages, out_ref = refs[:Y], refs[Y]
    count = messages[0].shape[0] - PACK - MOMENT_ROWS
    ranks = direction_ref.shape[0]
    rows = out_ref.shape[1] - 16
    direction = direction_ref[...]
    for d in range(Y):
        pieces = []
        for k in range(3):
            take = min(PACK, rows - k * PACK)
            pieces.append(messages[d][count : count + take, k * ranks : (k + 1) * ranks])
        basis = jnp.concatenate(pieces, 0)
        out_ref[source(at_ref[0], d), :rows, :] = jnp.dot(basis, direction, preferred_element_type=f32).astype(bf16)
    parts = jnp.concatenate(three_parts(gradient_ref[...]), 0).astype(bf16)
    shape = (Y * 16, parts.shape[0])
    row, column = lax.broadcasted_iota(jnp.int32, shape, 0), lax.broadcasted_iota(jnp.int32, shape, 1)
    place = row % 16
    wanted = place // 4 * gradient_ref.shape[0] + row // 16 * 4 + place % 4
    pick = ((column == wanted) & (place < 12)).astype(bf16)
    picked = jnp.dot(pick, parts, preferred_element_type=f32).astype(bf16)
    for y in range(Y):
        out_ref[y, rows:, :] = picked[16 * y : 16 * (y + 1), :]


def finish_kernel(at_ref, arrived_ref, first_ref, second_ref, new_first_ref, new_second_ref, update_ref):
    rows = update_ref.shape[0]
    part = arrived_ref.shape[2]
    for y in range(Y):
        columns = slice(y * part, (y + 1) * part)
        update_ref[:, columns] = arrived_ref[y, :rows, :].astype(f32)
        parts = arrived_ref[y, rows:, :].astype(f32)
        gradient = parts[0:4] + parts[4:8] + parts[8:12]
        new_first, new_second = adam(first_ref[:, columns], second_ref[:, columns], gradient)
        new_first_ref[:, columns] = new_first
        new_second_ref[:, columns] = new_second


def on_device(tokens, basis, grad_out, first_moment, second_moment):
    rows, ranks = basis.shape
    count, features = tokens.shape
    share, columns = first_moment.shape
    part = columns // Y
    half = ranks // C
    core = lax.axis_index("c")
    at = jnp.stack([lax.axis_index("y"), core])

    ordered_half = jnp.dot(basis, rank_order(core * half, half, ranks), preferred_element_type=f32).astype(bf16)
    turned = lax.ppermute(ordered_half, ("y", "x"), [(y * X + x, x * X + y) for y in range(Y) for x in range(X)])
    chip_basis = gather(turned, "z", Z).reshape(C, features, half)

    other = lax.ppermute(tokens, "c", [(0, 1), (1, 0)])

    ordered = jnp.dot(basis, rank_order(0, ranks, ranks), preferred_element_type=f32).astype(bf16)
    moments = jnp.concatenate([first_moment, second_moment], 0)
    message = (count + PACK + MOMENT_ROWS, part)
    messages = call(pack_kernel, "pack", [(message, bf16)] * Y, at, ordered, grad_out, moments)
    sent = {d: send(messages[d], d) for d in (2, 3, 1)}

    (summands,) = call(project_kernel, "project", [((X, count, half), f32)], at, tokens, other, chip_basis)
    summands = exchange(summands, "x")
    (projected,) = call(round_kernel, "round", [((C * Y, count, half), bf16)], at, summands)
    projected, sent[2], sent[3], sent[1] = lax.optimization_barrier((projected, sent[2], sent[3], sent[1]))
    messages = [messages[0], sent[1], sent[2], sent[3]]
    first, second = call(moments_kernel, "moments", [((ranks // Z, part), f32)] * 2, at, *messages)
    projected, first, second = lax.optimization_barrier((projected, first, second))
    projected = exchange(projected, ("c", "y")).reshape(C, Y, count, half)

    (partial,) = call(partial_kernel, "partial", [((ranks, part), bf16)], at, projected, *messages)
    pieces = exchange(partial.reshape(Z, ranks // Z, part), "z")
    gradient, direction = call(
        adam_kernel,
        "sum_and_adam",
        [((ranks // Z, part), f32), ((Z, ranks // Z, part), bf16)],
        at,
        pieces,
        first,
        second,
    )
    direction = exchange(direction, "z").reshape(ranks, part)
    (update,) = call(update_kernel, "update", [((Y, rows + 16, part), bf16)], at, direction, gradient, *messages)
    arrived = exchange(update, "y")
    return tuple(
        call(
            finish_kernel,
            "finish",
            [((share, columns), f32), ((share, columns), f32), ((rows, columns), f32)],
            at,
            arrived,
            first_moment,
            second_moment,
        )
    )


def solution(mesh):
    grid = Mesh(mesh.devices.reshape(Y, Z, X, C), ("y", "z", "x", "c"))
    dp, col = ("y", "z"), ("x", "c")
    return jax.shard_map(
        on_device,
        mesh=grid,
        in_specs=(P(dp, col), P(dp, None), P(dp, col), P(dp, col), P(dp, col)),
        out_specs=(P(dp, col), P(dp, col), P(dp, col)),
        check_vma=False,
    )
```

```python
import jax
import jax.numpy as jnp
from jax import lax
from jax.experimental import pallas as pl
from jax.experimental.pallas import tpu as pltpu
from jax.sharding import Mesh, PartitionSpec as P

STEP = 10
Y, H, L, X, C = 4, 8, 2, 4, 2
Z = H * L
PACK = 48
MOMENT_ROWS = 32
bf16, f32 = jnp.bfloat16, jnp.float32
TURN = [(x * X + (y + 2) % X, y * X + x) for y in range(Y) for x in range(X)]
VMEM = pl.BlockSpec(memory_space=pltpu.VMEM)
SMEM = pl.BlockSpec(memory_space=pltpu.SMEM)


def exchange(x, axes):
    return lax.all_to_all(x, axes, 0, 0, tiled=True)


def gather(x, axes, n):
    return exchange(jnp.broadcast_to(x[None], (n,) + x.shape), axes)


def send(x, step):
    return lax.ppermute(x, "y", [(y, (y + step) % Y) for y in range(Y)])


def call(kernel, name, out, *args):
    return pl.pallas_call(
        kernel,
        out_shape=[jax.ShapeDtypeStruct(shape, dtype) for shape, dtype in out],
        in_specs=[SMEM] + [VMEM] * (len(args) - 1),
        out_specs=[VMEM] * len(out),
        compiler_params=pltpu.CompilerParams(vmem_limit_bytes=32 * 2**20),
        name=name,
    )(*args)


def rank_order(first, count, ranks):
    share = ranks // (Y * Z)
    place = lax.broadcasted_iota(jnp.int32, (ranks, count), 1) + first
    z, y, j = place // (Y * share), place // share % Y, place % share
    rank = (y * Z + z) * share + j
    return (lax.broadcasted_iota(jnp.int32, (ranks, count), 0) == rank).astype(bf16)


def three_parts(x):
    high = x.astype(bf16).astype(f32)
    rest = x - high
    middle = rest.astype(bf16).astype(f32)
    return high, middle, rest - middle


def adam(first_moment, second_moment, gradient):
    new_first = 0.9 * first_moment + 0.1 * gradient
    new_second = 0.999 * second_moment + 0.001 * gradient * gradient
    return new_first, new_second


def source(me, d):
    return (me + Y - d) & (Y - 1)


def pack_kernel(at_ref, basis_ref, moments_ref, grad_ref, *refs):
    outs, (rest_ref, done_ref) = refs[:Y], refs[Y:]
    part = outs[0].shape[1]
    count = grad_ref.shape[0]
    rows, ranks = basis_ref.shape
    begins = [pl.multiple_of(((at_ref[0] + d) & (Y - 1)) * part, 128) for d in range(Y)]
    order = (2, 3, 1, 0)
    copies = []
    for d in order:
        block = grad_ref.at[:, pl.ds(begins[d], part)]
        copies.append(pltpu.make_async_copy(block, outs[d].at[pl.ds(0, count), :], done_ref.at[d]))
        copies[-1].start()
    for d in order:
        for k in range(3):
            take = min(PACK, rows - k * PACK)
            rest_ref[d, :take, k * ranks : (k + 1) * ranks] = basis_ref[k * PACK : k * PACK + take, :]
        parts = three_parts(moments_ref[:, pl.ds(begins[d], part)])
        parts = jnp.concatenate(parts + (jnp.zeros_like(parts[0]),), 0)
        rest_ref[d, PACK:, :] = parts.astype(bf16)
        rest = outs[d].at[pl.ds(count, PACK + MOMENT_ROWS), :]
        copies.append(pltpu.make_async_copy(rest_ref.at[d], rest, done_ref.at[Y + d]))
        copies[-1].start()
    for copy in copies:
        copy.wait()


def project_kernel(at_ref, tokens_ref, other_ref, own_ref, got_ref, out_ref):
    core, l = at_ref[1], at_ref[2]
    shards, block, half = own_ref.shape
    total = 0.0
    for c, part_ref in ((core, tokens_ref), (1 - core, other_ref)):
        for parity, basis_ref in ((l, own_ref), (1 - l, got_ref)):
            pieces = []
            for b in range(shards // C):
                begin = pl.multiple_of((L * b + parity) * block, block)
                pieces.append(part_ref[:, pl.ds(begin, block)])
            rows = jnp.concatenate([basis_ref[c * (shards // C) + b] for b in range(shards // C)], 0)
            total += jnp.dot(jnp.concatenate(pieces, 1), rows, preferred_element_type=f32)
    for x in range(out_ref.shape[0]):
        out_ref[x] = total


def round_kernel(at_ref, summands_ref, out_ref):
    total = jnp.sum(summands_ref[...], axis=0).astype(bf16)
    for i in range(out_ref.shape[0]):
        out_ref[i] = total


def partial_kernel(at_ref, projected_ref, *refs):
    messages, out_ref = refs[:Y], refs[Y]
    count, half = projected_ref.shape[2:]
    for c in range(C):
        total = 0.0
        for d in range(Y):
            tokens = projected_ref[c, source(at_ref[0], d)]
            total += lax.dot_general(tokens, messages[d][:count, :], (((0,), (0,)), ((), ())), preferred_element_type=f32)
        out_ref[c * half : (c + 1) * half, :] = total.astype(bf16)


def moments_of(at_ref, messages, ranks):
    stack = jnp.concatenate([m[m.shape[0] - MOMENT_ROWS :, :] for m in messages], 0)
    shape = (6 * ranks, stack.shape[0])
    row, column = lax.broadcasted_iota(jnp.int32, shape, 0), lax.broadcasted_iota(jnp.int32, shape, 1)
    which, rank = row // ranks, row % ranks
    moment, piece = which // 3, which % 3
    block = (at_ref[0] + Y - rank // 4) & (Y - 1)
    pick = (column == block * MOMENT_ROWS + piece * 8 + moment * 4 + rank % 4).astype(bf16)
    picked = jnp.dot(pick, stack, preferred_element_type=f32)
    for m in range(2):
        high, middle, low = (picked[(3 * m + p) * ranks : (3 * m + p + 1) * ranks, :] for p in range(3))
        yield high + middle + low


def adam_kernel(at_ref, pieces_ref, *refs):
    messages, (gradient_ref, direction_ref) = refs[:Y], refs[Y:]
    gradient = jnp.sum(pieces_ref[...].astype(f32), axis=0)
    gradient_ref[...] = gradient
    first_scale = 1.0 - 0.9**STEP
    second_scale = 1.0 - 0.999**STEP
    new_first, new_second = adam(*moments_of(at_ref, messages, gradient.shape[0]), gradient)
    direction = new_first / first_scale / (jnp.sqrt(new_second / second_scale) + 1e-08)
    direction = direction.astype(bf16)
    for h in range(direction_ref.shape[0]):
        direction_ref[h] = direction


def update_kernel(at_ref, direction_ref, gradient_ref, *refs):
    messages, out_ref = refs[:Y], refs[Y]
    count = messages[0].shape[0] - PACK - MOMENT_ROWS
    ranks = direction_ref.shape[0]
    rows = out_ref.shape[1] - 16
    direction = direction_ref[...]
    for d in range(Y):
        pieces = []
        for k in range(3):
            take = min(PACK, rows - k * PACK)
            pieces.append(messages[d][count : count + take, k * ranks : (k + 1) * ranks])
        basis = jnp.concatenate(pieces, 0)
        out_ref[source(at_ref[0], d), :rows, :] = jnp.dot(basis, direction, preferred_element_type=f32).astype(bf16)
    parts = jnp.concatenate(three_parts(gradient_ref[...]), 0).astype(bf16)
    shape = (Y * 16, parts.shape[0])
    row, column = lax.broadcasted_iota(jnp.int32, shape, 0), lax.broadcasted_iota(jnp.int32, shape, 1)
    place = row % 16
    wanted = place // 4 * gradient_ref.shape[0] + row // 16 * 4 + place % 4
    pick = ((column == wanted) & (place < 12)).astype(bf16)
    picked = jnp.dot(pick, parts, preferred_element_type=f32).astype(bf16)
    for y in range(Y):
        out_ref[y, rows:, :] = picked[16 * y : 16 * (y + 1), :]


def finish_kernel(at_ref, arrived_ref, first_ref, second_ref, new_first_ref, new_second_ref, update_ref):
    rows = update_ref.shape[0]
    part = arrived_ref.shape[2]
    for y in range(Y):
        columns = slice(y * part, (y + 1) * part)
        update_ref[:, columns] = arrived_ref[y, :rows, :].astype(f32)
        parts = arrived_ref[y, rows:, :].astype(f32)
        gradient = parts[0:4] + parts[4:8] + parts[8:12]
        new_first, new_second = adam(first_ref[:, columns], second_ref[:, columns], gradient)
        new_first_ref[:, columns] = new_first
        new_second_ref[:, columns] = new_second


def on_device(tokens, basis, grad_out, first_moment, second_moment):
    rows, ranks = basis.shape
    count, features = tokens.shape
    share, columns = first_moment.shape
    part = columns // Y
    half = ranks // C
    core = lax.axis_index("c")
    at = jnp.stack([lax.axis_index("y"), core, lax.axis_index("l")])

    ordered_half = jnp.dot(basis, rank_order(core * half, half, ranks), preferred_element_type=f32).astype(bf16)
    turned = lax.ppermute(ordered_half, ("y", "x"), TURN)
    own_basis = gather(turned, "h", H)
    got_basis = lax.ppermute(own_basis, "l", [(0, 1), (1, 0)])

    ordered = jnp.dot(basis, rank_order(0, ranks, ranks), preferred_element_type=f32).astype(bf16)
    moments = jnp.concatenate([first_moment, second_moment], 0)
    message = (count + PACK + MOMENT_ROWS, part)
    anywhere = pl.BlockSpec(memory_space=pl.ANY)
    messages = pl.pallas_call(
        pack_kernel,
        out_shape=[jax.ShapeDtypeStruct(message, bf16)] * Y,
        in_specs=[SMEM, VMEM, VMEM, anywhere],
        out_specs=[anywhere] * Y,
        scratch_shapes=[pltpu.VMEM((Y, PACK + MOMENT_ROWS, part), bf16), pltpu.SemaphoreType.DMA((2 * Y,))],
        compiler_params=pltpu.CompilerParams(vmem_limit_bytes=32 * 2**20),
        name="pack",
    )(at, ordered, moments, grad_out)
    sent = {d: send(messages[d], d) for d in (2, 3, 1)}

    tokens, first_message = lax.optimization_barrier((tokens, messages[0]))
    other = lax.ppermute(tokens, "c", [(0, 1), (1, 0)])

    (summands,) = call(project_kernel, "project", [((X, count, half), f32)], at, tokens, other, own_basis, got_basis)
    summands, sent[2] = lax.optimization_barrier((summands, sent[2]))
    summands = exchange(summands, "x")
    (projected,) = call(round_kernel, "round", [((C * Y, count, half), bf16)], at, summands)
    projected, sent[3], sent[1] = lax.optimization_barrier((projected, sent[3], sent[1]))
    messages = [first_message, sent[1], sent[2], sent[3]]
    projected = exchange(projected, ("c", "y")).reshape(C, Y, count, half)

    (partial,) = call(partial_kernel, "partial", [((ranks, part), bf16)], at, projected, *messages)
    pieces = exchange(partial.reshape(Z, ranks // Z, part), ("h", "l"))
    gradient, direction = call(
        adam_kernel,
        "sum_and_adam",
        [((ranks // Z, part), f32), ((Z, ranks // Z, part), bf16)],
        at,
        pieces,
        *messages,
    )
    direction = exchange(direction, ("h", "l")).reshape(ranks, part)
    (update,) = call(update_kernel, "update", [((Y, rows + 16, part), bf16)], at, direction, gradient, *messages)
    arrived = exchange(update, "y")
    return tuple(
        call(
            finish_kernel,
            "finish",
            [((share, columns), f32), ((share, columns), f32), ((rows, columns), f32)],
            at,
            arrived,
            first_moment,
            second_moment,
        )
    )


def solution(mesh):
    grid = Mesh(mesh.devices.reshape(Y, H, L, X, C), ("y", "h", "l", "x", "c"))
    dp, col = ("y", "h", "l"), ("x", "c")
    return jax.shard_map(
        on_device,
        mesh=grid,
        in_specs=(P(dp, col), P(dp, None), P(dp, col), P(dp, col), P(dp, col)),
        out_specs=(P(dp, col), P(dp, col), P(dp, col)),
        check_vma=False,
    )
```

```python
import jax
import jax.numpy as jnp
from jax import lax
from jax.experimental import pallas as pl
from jax.experimental.pallas import tpu as pltpu
from jax.sharding import Mesh, PartitionSpec as P

STEP = 10
Y, H, L, X, C = 4, 8, 2, 4, 2
Z = H * L
PACK = 48
MOMENT_ROWS = 32
bf16, f32 = jnp.bfloat16, jnp.float32
TURN = [(x * X + (y + 2) % X, y * X + x) for y in range(Y) for x in range(X)]
VMEM = pl.BlockSpec(memory_space=pltpu.VMEM)
SMEM = pl.BlockSpec(memory_space=pltpu.SMEM)


def exchange(x, axes):
    return lax.all_to_all(x, axes, 0, 0, tiled=True)


def gather(x, axes, n):
    return exchange(jnp.broadcast_to(x[None], (n,) + x.shape), axes)


def send(x, step):
    return lax.ppermute(x, "y", [(y, (y + step) % Y) for y in range(Y)])


def call(kernel, name, out, *args):
    return pl.pallas_call(
        kernel,
        out_shape=[jax.ShapeDtypeStruct(shape, dtype) for shape, dtype in out],
        in_specs=[SMEM] + [VMEM] * (len(args) - 1),
        out_specs=[VMEM] * len(out),
        compiler_params=pltpu.CompilerParams(vmem_limit_bytes=32 * 2**20),
        name=name,
    )(*args)


def rank_order(first, count, ranks):
    share = ranks // (Y * Z)
    place = lax.broadcasted_iota(jnp.int32, (ranks, count), 1) + first
    z, y, j = place // (Y * share), place // share % Y, place % share
    rank = (y * Z + z) * share + j
    return (lax.broadcasted_iota(jnp.int32, (ranks, count), 0) == rank).astype(bf16)


def three_parts(x):
    high = x.astype(bf16).astype(f32)
    rest = x - high
    middle = rest.astype(bf16).astype(f32)
    return high, middle, rest - middle


def adam(first_moment, second_moment, gradient):
    new_first = 0.9 * first_moment + 0.1 * gradient
    new_second = 0.999 * second_moment + 0.001 * gradient * gradient
    return new_first, new_second


def source(me, d):
    return (me + Y - d) & (Y - 1)


def pack_kernel(at_ref, basis_ref, moments_ref, grad_ref, *refs):
    outs, (rest_ref, done_ref) = refs[:Y], refs[Y:]
    part = outs[0].shape[1]
    count = grad_ref.shape[0]
    rows, ranks = basis_ref.shape
    begins = [pl.multiple_of(((at_ref[0] + d) & (Y - 1)) * part, 128) for d in range(Y)]
    order = (2, 3, 1, 0)
    copies = []
    for d in order:
        block = grad_ref.at[:, pl.ds(begins[d], part)]
        copies.append(pltpu.make_async_copy(block, outs[d].at[pl.ds(0, count), :], done_ref.at[d]))
        copies[-1].start()
    for d in order:
        for k in range(3):
            take = min(PACK, rows - k * PACK)
            rest_ref[d, :take, k * ranks : (k + 1) * ranks] = basis_ref[k * PACK : k * PACK + take, :]
        parts = three_parts(moments_ref[:, pl.ds(begins[d], part)])
        parts = jnp.concatenate(parts + (jnp.zeros_like(parts[0]),), 0)
        rest_ref[d, PACK:, :] = parts.astype(bf16)
        rest = outs[d].at[pl.ds(count, PACK + MOMENT_ROWS), :]
        copies.append(pltpu.make_async_copy(rest_ref.at[d], rest, done_ref.at[Y + d]))
        copies[-1].start()
    for copy in copies:
        copy.wait()


def project_kernel(at_ref, tokens_ref, other_ref, own_ref, got_ref, out_ref):
    core, l = at_ref[1], at_ref[2]
    shards, block, half = own_ref.shape
    total = 0.0
    for c, part_ref in ((core, tokens_ref), (1 - core, other_ref)):
        for parity, basis_ref in ((l, own_ref), (1 - l, got_ref)):
            pieces = []
            for b in range(shards // C):
                begin = pl.multiple_of((L * b + parity) * block, block)
                pieces.append(part_ref[:, pl.ds(begin, block)])
            rows = jnp.concatenate([basis_ref[c * (shards // C) + b] for b in range(shards // C)], 0)
            total += jnp.dot(jnp.concatenate(pieces, 1), rows, preferred_element_type=f32)
    for x in range(out_ref.shape[0]):
        out_ref[x] = total


def round_kernel(at_ref, summands_ref, out_ref):
    total = jnp.sum(summands_ref[...], axis=0).astype(bf16)
    for i in range(out_ref.shape[0]):
        out_ref[i] = total


def partial_kernel(at_ref, projected_ref, *refs):
    messages, out_ref = refs[:Y], refs[Y]
    count, half = projected_ref.shape[2:]
    for c in range(C):
        total = 0.0
        for d in range(Y):
            tokens = projected_ref[c, source(at_ref[0], d)]
            total += lax.dot_general(tokens, messages[d][:count, :], (((0,), (0,)), ((), ())), preferred_element_type=f32)
        out_ref[c * half : (c + 1) * half, :] = total.astype(bf16)


def moments_of(at_ref, messages, ranks):
    stack = jnp.concatenate([m[m.shape[0] - MOMENT_ROWS :, :] for m in messages], 0)
    shape = (6 * ranks, stack.shape[0])
    row, column = lax.broadcasted_iota(jnp.int32, shape, 0), lax.broadcasted_iota(jnp.int32, shape, 1)
    which, rank = row // ranks, row % ranks
    moment, piece = which // 3, which % 3
    block = (at_ref[0] + Y - rank // 4) & (Y - 1)
    pick = (column == block * MOMENT_ROWS + piece * 8 + moment * 4 + rank % 4).astype(bf16)
    picked = jnp.dot(pick, stack, preferred_element_type=f32)
    for m in range(2):
        high, middle, low = (picked[(3 * m + p) * ranks : (3 * m + p + 1) * ranks, :] for p in range(3))
        yield high + middle + low


def adam_kernel(at_ref, pieces_ref, *refs):
    messages, (gradient_ref, direction_ref) = refs[:Y], refs[Y:]
    gradient = jnp.sum(pieces_ref[...].astype(f32), axis=0)
    gradient_ref[...] = gradient
    first_scale = 1.0 - 0.9**STEP
    second_scale = 1.0 - 0.999**STEP
    new_first, new_second = adam(*moments_of(at_ref, messages, gradient.shape[0]), gradient)
    direction = new_first / first_scale / (jnp.sqrt(new_second / second_scale) + 1e-08)
    direction_ref[...] = direction.astype(bf16)


def update_kernel(at_ref, direction_ref, gradient_ref, *refs):
    messages, out_ref = refs[:Y], refs[Y]
    count = messages[0].shape[0] - PACK - MOMENT_ROWS
    ranks = direction_ref.shape[0]
    rows = out_ref.shape[1] - 16
    direction = direction_ref[...]
    for d in range(Y):
        pieces = []
        for k in range(3):
            take = min(PACK, rows - k * PACK)
            pieces.append(messages[d][count : count + take, k * ranks : (k + 1) * ranks])
        basis = jnp.concatenate(pieces, 0)
        out_ref[source(at_ref[0], d), :rows, :] = jnp.dot(basis, direction, preferred_element_type=f32).astype(bf16)
    parts = jnp.concatenate(three_parts(gradient_ref[...]), 0).astype(bf16)
    shape = (Y * 16, parts.shape[0])
    row, column = lax.broadcasted_iota(jnp.int32, shape, 0), lax.broadcasted_iota(jnp.int32, shape, 1)
    place = row % 16
    wanted = place // 4 * gradient_ref.shape[0] + row // 16 * 4 + place % 4
    pick = ((column == wanted) & (place < 12)).astype(bf16)
    picked = jnp.dot(pick, parts, preferred_element_type=f32).astype(bf16)
    for y in range(Y):
        out_ref[y, rows:, :] = picked[16 * y : 16 * (y + 1), :]


def finish_kernel(at_ref, arrived_ref, first_ref, second_ref, new_first_ref, new_second_ref, update_ref):
    rows = update_ref.shape[0]
    part = arrived_ref.shape[2]
    for y in range(Y):
        columns = slice(y * part, (y + 1) * part)
        update_ref[:, columns] = arrived_ref[y, :rows, :].astype(f32)
        parts = arrived_ref[y, rows:, :].astype(f32)
        gradient = parts[0:4] + parts[4:8] + parts[8:12]
        new_first, new_second = adam(first_ref[:, columns], second_ref[:, columns], gradient)
        new_first_ref[:, columns] = new_first
        new_second_ref[:, columns] = new_second


def on_device(tokens, basis, grad_out, first_moment, second_moment):
    rows, ranks = basis.shape
    count, features = tokens.shape
    share, columns = first_moment.shape
    part = columns // Y
    half = ranks // C
    core = lax.axis_index("c")
    at = jnp.stack([lax.axis_index("y"), core, lax.axis_index("l")])

    ordered_half = jnp.dot(basis, rank_order(core * half, half, ranks), preferred_element_type=f32).astype(bf16)
    turned = lax.ppermute(ordered_half, ("y", "x"), TURN)
    own_basis = gather(turned, "h", H)
    got_basis = lax.ppermute(own_basis, "l", [(0, 1), (1, 0)])

    ordered = jnp.dot(basis, rank_order(0, ranks, ranks), preferred_element_type=f32).astype(bf16)
    moments = jnp.concatenate([first_moment, second_moment], 0)
    message = (count + PACK + MOMENT_ROWS, part)
    anywhere = pl.BlockSpec(memory_space=pl.ANY)
    messages = pl.pallas_call(
        pack_kernel,
        out_shape=[jax.ShapeDtypeStruct(message, bf16)] * Y,
        in_specs=[SMEM, VMEM, VMEM, anywhere],
        out_specs=[anywhere] * Y,
        scratch_shapes=[pltpu.VMEM((Y, PACK + MOMENT_ROWS, part), bf16), pltpu.SemaphoreType.DMA((2 * Y,))],
        compiler_params=pltpu.CompilerParams(vmem_limit_bytes=32 * 2**20),
        name="pack",
    )(at, ordered, moments, grad_out)
    sent = {d: send(messages[d], d) for d in (2, 3, 1)}

    tokens, first_message = lax.optimization_barrier((tokens, messages[0]))
    other = lax.ppermute(tokens, "c", [(0, 1), (1, 0)])

    (summands,) = call(project_kernel, "project", [((X, count, half), f32)], at, tokens, other, own_basis, got_basis)
    summands, sent[2] = lax.optimization_barrier((summands, sent[2]))
    summands = exchange(summands, "x")
    (projected,) = call(round_kernel, "round", [((C * Y, count, half), bf16)], at, summands)
    projected, sent[3], sent[1] = lax.optimization_barrier((projected, sent[3], sent[1]))
    messages = [first_message, sent[1], sent[2], sent[3]]
    projected = exchange(projected, ("c", "y")).reshape(C, Y, count, half)

    (partial,) = call(partial_kernel, "partial", [((ranks, part), bf16)], at, projected, *messages)
    pieces = exchange(partial.reshape(Z, ranks // Z, part), ("h", "l"))
    gradient, direction = call(
        adam_kernel,
        "sum_and_adam",
        [((ranks // Z, part), f32), ((ranks // Z, part), bf16)],
        at,
        pieces,
        *messages,
    )
    direction = lax.all_gather(direction, ("h", "l"), axis=0, tiled=True)
    (update,) = call(update_kernel, "update", [((Y, rows + 16, part), bf16)], at, direction, gradient, *messages)
    arrived = exchange(update, "y")
    return tuple(
        call(
            finish_kernel,
            "finish",
            [((share, columns), f32), ((share, columns), f32), ((rows, columns), f32)],
            at,
            arrived,
            first_moment,
            second_moment,
        )
    )


def solution(mesh):
    grid = Mesh(mesh.devices.reshape(Y, H, L, X, C), ("y", "h", "l", "x", "c"))
    dp, col = ("y", "h", "l"), ("x", "c")
    return jax.shard_map(
        on_device,
        mesh=grid,
        in_specs=(P(dp, col), P(dp, None), P(dp, col), P(dp, col), P(dp, col)),
        out_specs=(P(dp, col), P(dp, col), P(dp, col)),
        check_vma=False,
    )
```

```python
import jax
import jax.numpy as jnp
from jax import lax
from jax.experimental import pallas as pl
from jax.experimental.pallas import tpu as pltpu
from jax.sharding import Mesh, PartitionSpec as P

STEP = 10
Y, H, L, X, C = 4, 8, 2, 4, 2
Z = H * L
PACK = 48
MOMENT_ROWS = 32
bf16, f32 = jnp.bfloat16, jnp.float32
TURN = [(x * X + (y + 2) % X, y * X + x) for y in range(Y) for x in range(X)]
VMEM = pl.BlockSpec(memory_space=pltpu.VMEM)
SMEM = pl.BlockSpec(memory_space=pltpu.SMEM)


def exchange(x, axes):
    return lax.all_to_all(x, axes, 0, 0, tiled=True)


def gather(x, axes, n):
    return exchange(jnp.broadcast_to(x[None], (n,) + x.shape), axes)


def send(x, step):
    return lax.ppermute(x, "y", [(y, (y + step) % Y) for y in range(Y)])


def send_one_core(x, step, c):
    return lax.ppermute(x, ("y", "c"), [(y * C + c, (y + step) % Y * C + c) for y in range(Y)])


def call(kernel, name, out, *args):
    return pl.pallas_call(
        kernel,
        out_shape=[jax.ShapeDtypeStruct(shape, dtype) for shape, dtype in out],
        in_specs=[SMEM] + [VMEM] * (len(args) - 1),
        out_specs=[VMEM] * len(out),
        compiler_params=pltpu.CompilerParams(vmem_limit_bytes=32 * 2**20),
        name=name,
    )(*args)


def rank_order(first, count, ranks):
    share = ranks // (Y * Z)
    place = lax.broadcasted_iota(jnp.int32, (ranks, count), 1) + first
    z, y, j = place // (Y * share), place // share % Y, place % share
    rank = (y * Z + z) * share + j
    return (lax.broadcasted_iota(jnp.int32, (ranks, count), 0) == rank).astype(bf16)


def three_parts(x):
    high = x.astype(bf16).astype(f32)
    rest = x - high
    middle = rest.astype(bf16).astype(f32)
    return high, middle, rest - middle


def adam(first_moment, second_moment, gradient):
    new_first = 0.9 * first_moment + 0.1 * gradient
    new_second = 0.999 * second_moment + 0.001 * gradient * gradient
    return new_first, new_second


def block_of(messages, d, rows, columns=slice(None)):
    block = messages[d][rows, columns]
    return block + messages[Y][rows, columns] if d == 1 else block


def source(me, d):
    return (me + Y - d) & (Y - 1)


def pack_kernel(at_ref, basis_ref, moments_ref, grad_ref, *refs):
    outs, (rest_ref, done_ref) = refs[:Y], refs[Y:]
    part = outs[0].shape[1]
    count = grad_ref.shape[0]
    rows, ranks = basis_ref.shape
    begins = [pl.multiple_of(((at_ref[0] + d) & (Y - 1)) * part, 128) for d in range(Y)]
    order = (2, 3, 1, 0)
    copies = []
    for d in order:
        block = grad_ref.at[:, pl.ds(begins[d], part)]
        copies.append(pltpu.make_async_copy(block, outs[d].at[pl.ds(0, count), :], done_ref.at[d]))
        copies[-1].start()
    for d in order:
        for k in range(3):
            take = min(PACK, rows - k * PACK)
            rest_ref[d, :take, k * ranks : (k + 1) * ranks] = basis_ref[k * PACK : k * PACK + take, :]
        parts = three_parts(moments_ref[:, pl.ds(begins[d], part)])
        parts = jnp.concatenate(parts + (jnp.zeros_like(parts[0]),), 0)
        rest_ref[d, PACK:, :] = parts.astype(bf16)
        rest = outs[d].at[pl.ds(count, PACK + MOMENT_ROWS), :]
        copies.append(pltpu.make_async_copy(rest_ref.at[d], rest, done_ref.at[Y + d]))
        copies[-1].start()
    for copy in copies:
        copy.wait()


def project_kernel(at_ref, tokens_ref, other_ref, own_ref, got_ref, out_ref):
    core, l = at_ref[1], at_ref[2]
    shards, block, half = own_ref.shape
    total = 0.0
    for c, part_ref in ((core, tokens_ref), (1 - core, other_ref)):
        for parity, basis_ref in ((l, own_ref), (1 - l, got_ref)):
            pieces = []
            for b in range(shards // C):
                begin = pl.multiple_of((L * b + parity) * block, block)
                pieces.append(part_ref[:, pl.ds(begin, block)])
            rows = jnp.concatenate([basis_ref[c * (shards // C) + b] for b in range(shards // C)], 0)
            total += jnp.dot(jnp.concatenate(pieces, 1), rows, preferred_element_type=f32)
    for x in range(out_ref.shape[0]):
        out_ref[x] = total


def round_kernel(at_ref, summands_ref, out_ref):
    total = jnp.sum(summands_ref[...], axis=0).astype(bf16)
    for i in range(out_ref.shape[0]):
        out_ref[i] = total


def partial_kernel(at_ref, projected_ref, *refs):
    messages, out_ref = refs[: Y + 1], refs[Y + 1]
    count, half = projected_ref.shape[2:]
    for c in range(C):
        total = 0.0
        for d in range(Y):
            tokens = projected_ref[c, source(at_ref[0], d)]
            total += lax.dot_general(tokens, block_of(messages, d, slice(0, count)), (((0,), (0,)), ((), ())), preferred_element_type=f32)
        out_ref[c * half : (c + 1) * half, :] = total.astype(bf16)


def moments_of(at_ref, messages, ranks):
    total = messages[0].shape[0]
    stack = jnp.concatenate([block_of(messages, d, slice(total - MOMENT_ROWS, total)) for d in range(Y)], 0)
    shape = (6 * ranks, stack.shape[0])
    row, column = lax.broadcasted_iota(jnp.int32, shape, 0), lax.broadcasted_iota(jnp.int32, shape, 1)
    which, rank = row // ranks, row % ranks
    moment, piece = which // 3, which % 3
    block = (at_ref[0] + Y - rank // 4) & (Y - 1)
    pick = (column == block * MOMENT_ROWS + piece * 8 + moment * 4 + rank % 4).astype(bf16)
    picked = jnp.dot(pick, stack, preferred_element_type=f32)
    for m in range(2):
        high, middle, low = (picked[(3 * m + p) * ranks : (3 * m + p + 1) * ranks, :] for p in range(3))
        yield high + middle + low


def adam_kernel(at_ref, pieces_ref, *refs):
    messages, (gradient_ref, direction_ref) = refs[: Y + 1], refs[Y + 1 :]
    gradient = jnp.sum(pieces_ref[...].astype(f32), axis=0)
    gradient_ref[...] = gradient
    first_scale = 1.0 - 0.9**STEP
    second_scale = 1.0 - 0.999**STEP
    new_first, new_second = adam(*moments_of(at_ref, messages, gradient.shape[0]), gradient)
    direction = new_first / first_scale / (jnp.sqrt(new_second / second_scale) + 1e-08)
    direction_ref[...] = direction.astype(bf16)


def update_kernel(at_ref, direction_ref, gradient_ref, *refs):
    messages, out_ref = refs[: Y + 1], refs[Y + 1]
    count = messages[0].shape[0] - PACK - MOMENT_ROWS
    ranks = direction_ref.shape[0]
    rows = out_ref.shape[1] - 16
    direction = direction_ref[...]
    for d in range(Y):
        pieces = []
        for k in range(3):
            take = min(PACK, rows - k * PACK)
            pieces.append(block_of(messages, d, slice(count, count + take), slice(k * ranks, (k + 1) * ranks)))
        basis = jnp.concatenate(pieces, 0)
        out_ref[source(at_ref[0], d), :rows, :] = jnp.dot(basis, direction, preferred_element_type=f32).astype(bf16)
    parts = jnp.concatenate(three_parts(gradient_ref[...]), 0).astype(bf16)
    shape = (Y * 16, parts.shape[0])
    row, column = lax.broadcasted_iota(jnp.int32, shape, 0), lax.broadcasted_iota(jnp.int32, shape, 1)
    place = row % 16
    wanted = place // 4 * gradient_ref.shape[0] + row // 16 * 4 + place % 4
    pick = ((column == wanted) & (place < 12)).astype(bf16)
    picked = jnp.dot(pick, parts, preferred_element_type=f32).astype(bf16)
    for y in range(Y):
        out_ref[y, rows:, :] = picked[16 * y : 16 * (y + 1), :]


def finish_kernel(at_ref, arrived_ref, first_ref, second_ref, new_first_ref, new_second_ref, update_ref):
    rows = update_ref.shape[0]
    part = arrived_ref.shape[2]
    for y in range(Y):
        columns = slice(y * part, (y + 1) * part)
        update_ref[:, columns] = arrived_ref[y, :rows, :].astype(f32)
        parts = arrived_ref[y, rows:, :].astype(f32)
        gradient = parts[0:4] + parts[4:8] + parts[8:12]
        new_first, new_second = adam(first_ref[:, columns], second_ref[:, columns], gradient)
        new_first_ref[:, columns] = new_first
        new_second_ref[:, columns] = new_second


def on_device(tokens, basis, grad_out, first_moment, second_moment):
    rows, ranks = basis.shape
    count, features = tokens.shape
    share, columns = first_moment.shape
    part = columns // Y
    half = ranks // C
    core = lax.axis_index("c")
    at = jnp.stack([lax.axis_index("y"), core, lax.axis_index("l")])

    ordered_half = jnp.dot(basis, rank_order(core * half, half, ranks), preferred_element_type=f32).astype(bf16)
    turned = lax.ppermute(ordered_half, ("y", "x"), TURN)
    own_basis = gather(turned, "h", H)
    got_basis = lax.ppermute(own_basis, "l", [(0, 1), (1, 0)])

    ordered = jnp.dot(basis, rank_order(0, ranks, ranks), preferred_element_type=f32).astype(bf16)
    moments = jnp.concatenate([first_moment, second_moment], 0)
    message = (count + PACK + MOMENT_ROWS, part)
    anywhere = pl.BlockSpec(memory_space=pl.ANY)
    messages = pl.pallas_call(
        pack_kernel,
        out_shape=[jax.ShapeDtypeStruct(message, bf16)] * Y,
        in_specs=[SMEM, VMEM, VMEM, anywhere],
        out_specs=[anywhere] * Y,
        scratch_shapes=[pltpu.VMEM((Y, PACK + MOMENT_ROWS, part), bf16), pltpu.SemaphoreType.DMA((2 * Y,))],
        compiler_params=pltpu.CompilerParams(vmem_limit_bytes=32 * 2**20),
        name="pack",
    )(at, ordered, moments, grad_out)
    sent = {2: send(messages[2], 2), 3: send(messages[3], 3), 1: send_one_core(messages[1], 1, 0)}
    late = messages[1]

    tokens, first_message = lax.optimization_barrier((tokens, messages[0]))
    other = lax.ppermute(tokens, "c", [(0, 1), (1, 0)])

    (summands,) = call(project_kernel, "project", [((X, count, half), f32)], at, tokens, other, own_basis, got_basis)
    summands, sent[2] = lax.optimization_barrier((summands, sent[2]))
    summands = exchange(summands, "x")
    (projected,) = call(round_kernel, "round", [((C * Y, count, half), bf16)], at, summands)
    projected, sent[3], sent[1] = lax.optimization_barrier((projected, sent[3], sent[1]))
    messages = [first_message, sent[1], sent[2], sent[3]]
    projected = exchange(projected, ("c", "y")).reshape(C, Y, count, half)
    projected, late = lax.optimization_barrier((projected, late))
    messages = messages + [send_one_core(late, 1, 1)]


    (partial,) = call(partial_kernel, "partial", [((ranks, part), bf16)], at, projected, *messages)
    pieces = exchange(partial.reshape(Z, ranks // Z, part), ("h", "l"))
    gradient, direction = call(
        adam_kernel,
        "sum_and_adam",
        [((ranks // Z, part), f32), ((ranks // Z, part), bf16)],
        at,
        pieces,
        *messages,
    )
    direction = lax.all_gather(direction, ("h", "l"), axis=0, tiled=True)
    (update,) = call(update_kernel, "update", [((Y, rows + 16, part), bf16)], at, direction, gradient, *messages)
    arrived = exchange(update, "y")
    return tuple(
        call(
            finish_kernel,
            "finish",
            [((share, columns), f32), ((share, columns), f32), ((rows, columns), f32)],
            at,
            arrived,
            first_moment,
            second_moment,
        )
    )


def solution(mesh):
    grid = Mesh(mesh.devices.reshape(Y, H, L, X, C), ("y", "h", "l", "x", "c"))
    dp, col = ("y", "h", "l"), ("x", "c")
    return jax.shard_map(
        on_device,
        mesh=grid,
        in_specs=(P(dp, col), P(dp, None), P(dp, col), P(dp, col), P(dp, col)),
        out_specs=(P(dp, col), P(dp, col), P(dp, col)),
        check_vma=False,
    )
```

```python
import jax
import jax.numpy as jnp
from jax import lax
from jax.experimental import pallas as pl
from jax.experimental.pallas import tpu as pltpu
from jax.sharding import Mesh, PartitionSpec as P

STEP = 10
Y, H, L, X, C = 4, 8, 2, 4, 2
Z = H * L
PACK = 48
MOMENT_ROWS = 32
bf16, f32 = jnp.bfloat16, jnp.float32
TURN = [(x * X + (y + 2) % X, y * X + x) for y in range(Y) for x in range(X)]
VMEM = pl.BlockSpec(memory_space=pltpu.VMEM)
SMEM = pl.BlockSpec(memory_space=pltpu.SMEM)


def exchange(x, axes):
    return lax.all_to_all(x, axes, 0, 0, tiled=True)


def gather(x, axes, n):
    return exchange(jnp.broadcast_to(x[None], (n,) + x.shape), axes)


def send(x, step):
    return lax.ppermute(x, "y", [(y, (y + step) % Y) for y in range(Y)])


def send_one_core(x, step, c):
    return lax.ppermute(x, ("y", "c"), [(y * C + c, (y + step) % Y * C + c) for y in range(Y)])


def call(kernel, name, out, *args):
    return pl.pallas_call(
        kernel,
        out_shape=[jax.ShapeDtypeStruct(shape, dtype) for shape, dtype in out],
        in_specs=[SMEM] + [VMEM] * (len(args) - 1),
        out_specs=[VMEM] * len(out),
        compiler_params=pltpu.CompilerParams(vmem_limit_bytes=32 * 2**20),
        name=name,
    )(*args)


def rank_order(first, count, ranks):
    share = ranks // (Y * Z)
    place = lax.broadcasted_iota(jnp.int32, (ranks, count), 1) + first
    z, y, j = place // (Y * share), place // share % Y, place % share
    rank = (y * Z + z) * share + j
    return (lax.broadcasted_iota(jnp.int32, (ranks, count), 0) == rank).astype(bf16)


def three_parts(x):
    high = x.astype(bf16).astype(f32)
    rest = x - high
    middle = rest.astype(bf16).astype(f32)
    return high, middle, rest - middle


def adam(first_moment, second_moment, gradient):
    new_first = 0.9 * first_moment + 0.1 * gradient
    new_second = 0.999 * second_moment + 0.001 * gradient * gradient
    return new_first, new_second


def block_of(messages, d, rows, columns=slice(None)):
    block = messages[d][rows, columns]
    return block + messages[Y][rows, columns] if d == 3 else block


def source(me, d):
    return (me + Y - d) & (Y - 1)


def pack_kernel(at_ref, basis_ref, moments_ref, grad_ref, *refs):
    outs, (rest_ref, done_ref) = refs[:Y], refs[Y:]
    part = outs[0].shape[1]
    count = grad_ref.shape[0]
    rows, ranks = basis_ref.shape
    begins = [pl.multiple_of(((at_ref[0] + d) & (Y - 1)) * part, 128) for d in range(Y)]
    order = (2, 3, 1, 0)
    copies = []
    for d in order:
        block = grad_ref.at[:, pl.ds(begins[d], part)]
        copies.append(pltpu.make_async_copy(block, outs[d].at[pl.ds(0, count), :], done_ref.at[d]))
        copies[-1].start()
    for d in order:
        for k in range(3):
            take = min(PACK, rows - k * PACK)
            rest_ref[d, :take, k * ranks : (k + 1) * ranks] = basis_ref[k * PACK : k * PACK + take, :]
        parts = three_parts(moments_ref[:, pl.ds(begins[d], part)])
        parts = jnp.concatenate(parts + (jnp.zeros_like(parts[0]),), 0)
        rest_ref[d, PACK:, :] = parts.astype(bf16)
        rest = outs[d].at[pl.ds(count, PACK + MOMENT_ROWS), :]
        copies.append(pltpu.make_async_copy(rest_ref.at[d], rest, done_ref.at[Y + d]))
        copies[-1].start()
    for copy in copies:
        copy.wait()


def project_kernel(at_ref, tokens_ref, other_ref, own_ref, got_ref, out_ref):
    core, l = at_ref[1], at_ref[2]
    shards, block, half = own_ref.shape
    total = 0.0
    for c, part_ref in ((core, tokens_ref), (1 - core, other_ref)):
        for parity, basis_ref in ((l, own_ref), (1 - l, got_ref)):
            pieces = []
            for b in range(shards // C):
                begin = pl.multiple_of((L * b + parity) * block, block)
                pieces.append(part_ref[:, pl.ds(begin, block)])
            rows = jnp.concatenate([basis_ref[c * (shards // C) + b] for b in range(shards // C)], 0)
            total += jnp.dot(jnp.concatenate(pieces, 1), rows, preferred_element_type=f32)
    for x in range(out_ref.shape[0]):
        out_ref[x] = total


def round_kernel(at_ref, summands_ref, out_ref):
    total = jnp.sum(summands_ref[...], axis=0).astype(bf16)
    for i in range(out_ref.shape[0]):
        out_ref[i] = total


def partial_kernel(at_ref, projected_ref, *refs):
    messages, out_ref = refs[: Y + 1], refs[Y + 1]
    count, half = projected_ref.shape[2:]
    for c in range(C):
        total = 0.0
        for d in range(Y):
            tokens = projected_ref[c, source(at_ref[0], d)]
            total += lax.dot_general(tokens, block_of(messages, d, slice(0, count)), (((0,), (0,)), ((), ())), preferred_element_type=f32)
        out_ref[c * half : (c + 1) * half, :] = total.astype(bf16)


def moments_of(at_ref, messages, ranks):
    total = messages[0].shape[0]
    stack = jnp.concatenate([block_of(messages, d, slice(total - MOMENT_ROWS, total)) for d in range(Y)], 0)
    shape = (6 * ranks, stack.shape[0])
    row, column = lax.broadcasted_iota(jnp.int32, shape, 0), lax.broadcasted_iota(jnp.int32, shape, 1)
    which, rank = row // ranks, row % ranks
    moment, piece = which // 3, which % 3
    block = (at_ref[0] + Y - rank // 4) & (Y - 1)
    pick = (column == block * MOMENT_ROWS + piece * 8 + moment * 4 + rank % 4).astype(bf16)
    picked = jnp.dot(pick, stack, preferred_element_type=f32)
    for m in range(2):
        high, middle, low = (picked[(3 * m + p) * ranks : (3 * m + p + 1) * ranks, :] for p in range(3))
        yield high + middle + low


def adam_kernel(at_ref, pieces_ref, *refs):
    messages, (gradient_ref, direction_ref) = refs[: Y + 1], refs[Y + 1 :]
    gradient = jnp.sum(pieces_ref[...].astype(f32), axis=0)
    gradient_ref[...] = gradient
    first_scale = 1.0 - 0.9**STEP
    second_scale = 1.0 - 0.999**STEP
    new_first, new_second = adam(*moments_of(at_ref, messages, gradient.shape[0]), gradient)
    direction = new_first / first_scale / (jnp.sqrt(new_second / second_scale) + 1e-08)
    direction_ref[...] = direction.astype(bf16)


def update_kernel(at_ref, direction_ref, gradient_ref, *refs):
    messages, out_ref = refs[: Y + 1], refs[Y + 1]
    count = messages[0].shape[0] - PACK - MOMENT_ROWS
    ranks = direction_ref.shape[0]
    rows = out_ref.shape[1] - 16
    direction = direction_ref[...]
    for d in range(Y):
        pieces = []
        for k in range(3):
            take = min(PACK, rows - k * PACK)
            pieces.append(block_of(messages, d, slice(count, count + take), slice(k * ranks, (k + 1) * ranks)))
        basis = jnp.concatenate(pieces, 0)
        out_ref[source(at_ref[0], d), :rows, :] = jnp.dot(basis, direction, preferred_element_type=f32).astype(bf16)
    parts = jnp.concatenate(three_parts(gradient_ref[...]), 0).astype(bf16)
    shape = (Y * 16, parts.shape[0])
    row, column = lax.broadcasted_iota(jnp.int32, shape, 0), lax.broadcasted_iota(jnp.int32, shape, 1)
    place = row % 16
    wanted = place // 4 * gradient_ref.shape[0] + row // 16 * 4 + place % 4
    pick = ((column == wanted) & (place < 12)).astype(bf16)
    picked = jnp.dot(pick, parts, preferred_element_type=f32).astype(bf16)
    for y in range(Y):
        out_ref[y, rows:, :] = picked[16 * y : 16 * (y + 1), :]


def finish_kernel(at_ref, arrived_ref, first_ref, second_ref, new_first_ref, new_second_ref, update_ref):
    rows = update_ref.shape[0]
    part = arrived_ref.shape[2]
    for y in range(Y):
        columns = slice(y * part, (y + 1) * part)
        update_ref[:, columns] = arrived_ref[y, :rows, :].astype(f32)
        parts = arrived_ref[y, rows:, :].astype(f32)
        gradient = parts[0:4] + parts[4:8] + parts[8:12]
        new_first, new_second = adam(first_ref[:, columns], second_ref[:, columns], gradient)
        new_first_ref[:, columns] = new_first
        new_second_ref[:, columns] = new_second


def on_device(tokens, basis, grad_out, first_moment, second_moment):
    rows, ranks = basis.shape
    count, features = tokens.shape
    share, columns = first_moment.shape
    part = columns // Y
    half = ranks // C
    core = lax.axis_index("c")
    at = jnp.stack([lax.axis_index("y"), core, lax.axis_index("l")])

    ordered_half = jnp.dot(basis, rank_order(core * half, half, ranks), preferred_element_type=f32).astype(bf16)
    turned = lax.ppermute(ordered_half, ("y", "x"), TURN)
    own_basis = gather(turned, "h", H)
    got_basis = lax.ppermute(own_basis, "l", [(0, 1), (1, 0)])

    ordered = jnp.dot(basis, rank_order(0, ranks, ranks), preferred_element_type=f32).astype(bf16)
    moments = jnp.concatenate([first_moment, second_moment], 0)
    message = (count + PACK + MOMENT_ROWS, part)
    anywhere = pl.BlockSpec(memory_space=pl.ANY)
    messages = pl.pallas_call(
        pack_kernel,
        out_shape=[jax.ShapeDtypeStruct(message, bf16)] * Y,
        in_specs=[SMEM, VMEM, VMEM, anywhere],
        out_specs=[anywhere] * Y,
        scratch_shapes=[pltpu.VMEM((Y, PACK + MOMENT_ROWS, part), bf16), pltpu.SemaphoreType.DMA((2 * Y,))],
        compiler_params=pltpu.CompilerParams(vmem_limit_bytes=32 * 2**20),
        name="pack",
    )(at, ordered, moments, grad_out)
    sent = {2: send(messages[2], 2), 1: send(messages[1], 1), 3: send_one_core(messages[3], 3, 0)}
    late = messages[3]

    tokens, first_message = lax.optimization_barrier((tokens, messages[0]))
    other = lax.ppermute(tokens, "c", [(0, 1), (1, 0)])

    (summands,) = call(project_kernel, "project", [((X, count, half), f32)], at, tokens, other, own_basis, got_basis)
    summands, sent[2] = lax.optimization_barrier((summands, sent[2]))
    summands = exchange(summands, "x")
    (projected,) = call(round_kernel, "round", [((C * Y, count, half), bf16)], at, summands)
    projected, sent[1], sent[3] = lax.optimization_barrier((projected, sent[1], sent[3]))
    messages = [first_message, sent[1], sent[2], sent[3]]
    projected = exchange(projected, ("c", "y")).reshape(C, Y, count, half)
    projected, late = lax.optimization_barrier((projected, late))
    messages = messages + [send_one_core(late, 3, 1)]


    (partial,) = call(partial_kernel, "partial", [((ranks, part), bf16)], at, projected, *messages)
    pieces = exchange(partial.reshape(Z, ranks // Z, part), ("h", "l"))
    gradient, direction = call(
        adam_kernel,
        "sum_and_adam",
        [((ranks // Z, part), f32), ((ranks // Z, part), bf16)],
        at,
        pieces,
        *messages,
    )
    direction = lax.all_gather(direction, ("h", "l"), axis=0, tiled=True)
    (update,) = call(update_kernel, "update", [((Y, rows + 16, part), bf16)], at, direction, gradient, *messages)
    arrived = exchange(update, "y")
    return tuple(
        call(
            finish_kernel,
            "finish",
            [((share, columns), f32), ((share, columns), f32), ((rows, columns), f32)],
            at,
            arrived,
            first_moment,
            second_moment,
        )
    )


def solution(mesh):
    grid = Mesh(mesh.devices.reshape(Y, H, L, X, C), ("y", "h", "l", "x", "c"))
    dp, col = ("y", "h", "l"), ("x", "c")
    return jax.shard_map(
        on_device,
        mesh=grid,
        in_specs=(P(dp, col), P(dp, None), P(dp, col), P(dp, col), P(dp, col)),
        out_specs=(P(dp, col), P(dp, col), P(dp, col)),
        check_vma=False,
    )
```

```python
import jax
import jax.numpy as jnp
from jax import lax
from jax.experimental import pallas as pl
from jax.experimental.pallas import tpu as pltpu
from jax.sharding import Mesh, PartitionSpec as P

STEP = 10
Y, H, L, X, C = 4, 8, 2, 4, 2
Z = H * L
PACK = 48
MOMENT_ROWS = 32
bf16, f32 = jnp.bfloat16, jnp.float32
TURN = [(x * X + (y + 2) % X, y * X + x) for y in range(Y) for x in range(X)]
VMEM = pl.BlockSpec(memory_space=pltpu.VMEM)
SMEM = pl.BlockSpec(memory_space=pltpu.SMEM)


def exchange(x, axes):
    return lax.all_to_all(x, axes, 0, 0, tiled=True)


def gather(x, axes, n):
    return exchange(jnp.broadcast_to(x[None], (n,) + x.shape), axes)


def send(x, step):
    return lax.ppermute(x, "y", [(y, (y + step) % Y) for y in range(Y)])


def send_one_core(x, step, c):
    return lax.ppermute(x, ("y", "c"), [(y * C + c, (y + step) % Y * C + c) for y in range(Y)])


def call(kernel, name, out, *args):
    return pl.pallas_call(
        kernel,
        out_shape=[jax.ShapeDtypeStruct(shape, dtype) for shape, dtype in out],
        in_specs=[SMEM] + [VMEM] * (len(args) - 1),
        out_specs=[VMEM] * len(out),
        compiler_params=pltpu.CompilerParams(vmem_limit_bytes=32 * 2**20),
        name=name,
    )(*args)


def rank_order(first, count, ranks):
    share = ranks // (Y * Z)
    place = lax.broadcasted_iota(jnp.int32, (ranks, count), 1) + first
    z, y, j = place // (Y * share), place // share % Y, place % share
    rank = (y * Z + z) * share + j
    return (lax.broadcasted_iota(jnp.int32, (ranks, count), 0) == rank).astype(bf16)


def three_parts(x):
    high = x.astype(bf16).astype(f32)
    rest = x - high
    middle = rest.astype(bf16).astype(f32)
    return high, middle, rest - middle


def adam(first_moment, second_moment, gradient):
    new_first = 0.9 * first_moment + 0.1 * gradient
    new_second = 0.999 * second_moment + 0.001 * gradient * gradient
    return new_first, new_second


def block_of(messages, d, rows, columns=slice(None)):
    block = messages[d][rows, columns]
    return block + messages[Y][rows, columns] if d == 3 else block


def source(me, d):
    return (me + Y - d) & (Y - 1)


def pack_kernel(at_ref, basis_ref, moments_ref, grad_ref, *refs):
    outs, (rest_ref, done_ref) = refs[:Y], refs[Y:]
    part = outs[0].shape[1]
    count = grad_ref.shape[0]
    rows, ranks = basis_ref.shape
    begins = [pl.multiple_of(((at_ref[0] + d) & (Y - 1)) * part, 128) for d in range(Y)]
    order = (2, 3, 1, 0)
    copies = []
    for d in order:
        block = grad_ref.at[:, pl.ds(begins[d], part)]
        copies.append(pltpu.make_async_copy(block, outs[d].at[pl.ds(0, count), :], done_ref.at[d]))
        copies[-1].start()
    for d in order:
        for k in range(3):
            take = min(PACK, rows - k * PACK)
            rest_ref[d, :take, k * ranks : (k + 1) * ranks] = basis_ref[k * PACK : k * PACK + take, :]
        parts = three_parts(moments_ref[:, pl.ds(begins[d], part)])
        parts = jnp.concatenate(parts + (jnp.zeros_like(parts[0]),), 0)
        rest_ref[d, PACK:, :] = parts.astype(bf16)
        rest = outs[d].at[pl.ds(count, PACK + MOMENT_ROWS), :]
        copies.append(pltpu.make_async_copy(rest_ref.at[d], rest, done_ref.at[Y + d]))
        copies[-1].start()
    for copy in copies:
        copy.wait()


def project_kernel(at_ref, tokens_ref, other_ref, own_ref, got_ref, out_ref):
    core, l = at_ref[1], at_ref[2]
    shards, block, half = own_ref.shape
    total = 0.0
    for c, part_ref in ((core, tokens_ref), (1 - core, other_ref)):
        for parity, basis_ref in ((l, own_ref), (1 - l, got_ref)):
            pieces = []
            for b in range(shards // C):
                begin = pl.multiple_of((L * b + parity) * block, block)
                pieces.append(part_ref[:, pl.ds(begin, block)])
            rows = jnp.concatenate([basis_ref[c * (shards // C) + b] for b in range(shards // C)], 0)
            total += jnp.dot(jnp.concatenate(pieces, 1), rows, preferred_element_type=f32)
    for x in range(out_ref.shape[0]):
        out_ref[x] = total


def round_kernel(at_ref, summands_ref, out_ref):
    total = jnp.sum(summands_ref[...], axis=0).astype(bf16)
    for i in range(out_ref.shape[0]):
        out_ref[i] = total


def early_kernel(at_ref, projected_ref, *refs):
    messages, out_ref = refs[:Y], refs[Y]
    count, half = projected_ref.shape[2:]
    for c in range(C):
        total = 0.0
        for d in range(Y):
            tokens = projected_ref[c, source(at_ref[0], d)]
            grads = messages[d][:count, :]
            total += lax.dot_general(tokens, grads, (((0,), (0,)), ((), ())), preferred_element_type=f32)
        out_ref[c * half : (c + 1) * half, :] = total


def late_kernel(at_ref, early_ref, projected_ref, late_ref, out_ref):
    count, half = projected_ref.shape[2:]
    for c in range(C):
        tokens = projected_ref[c, source(at_ref[0], 3)]
        total = lax.dot_general(tokens, late_ref[:count, :], (((0,), (0,)), ((), ())), preferred_element_type=f32)
        rows = slice(c * half, (c + 1) * half)
        out_ref[rows, :] = (early_ref[rows, :] + total).astype(bf16)


def moments_of(at_ref, messages, ranks):
    total = messages[0].shape[0]
    stack = jnp.concatenate([block_of(messages, d, slice(total - MOMENT_ROWS, total)) for d in range(Y)], 0)
    shape = (6 * ranks, stack.shape[0])
    row, column = lax.broadcasted_iota(jnp.int32, shape, 0), lax.broadcasted_iota(jnp.int32, shape, 1)
    which, rank = row // ranks, row % ranks
    moment, piece = which // 3, which % 3
    block = (at_ref[0] + Y - rank // 4) & (Y - 1)
    pick = (column == block * MOMENT_ROWS + piece * 8 + moment * 4 + rank % 4).astype(bf16)
    picked = jnp.dot(pick, stack, preferred_element_type=f32)
    for m in range(2):
        high, middle, low = (picked[(3 * m + p) * ranks : (3 * m + p + 1) * ranks, :] for p in range(3))
        yield high + middle + low


def adam_kernel(at_ref, pieces_ref, *refs):
    messages, (gradient_ref, direction_ref) = refs[: Y + 1], refs[Y + 1 :]
    gradient = jnp.sum(pieces_ref[...].astype(f32), axis=0)
    gradient_ref[...] = gradient
    first_scale = 1.0 - 0.9**STEP
    second_scale = 1.0 - 0.999**STEP
    new_first, new_second = adam(*moments_of(at_ref, messages, gradient.shape[0]), gradient)
    direction = new_first / first_scale / (jnp.sqrt(new_second / second_scale) + 1e-08)
    direction_ref[...] = direction.astype(bf16)


def update_kernel(at_ref, direction_ref, gradient_ref, *refs):
    messages, out_ref = refs[: Y + 1], refs[Y + 1]
    count = messages[0].shape[0] - PACK - MOMENT_ROWS
    ranks = direction_ref.shape[0]
    rows = out_ref.shape[1] - 16
    direction = direction_ref[...]
    for d in range(Y):
        pieces = []
        for k in range(3):
            take = min(PACK, rows - k * PACK)
            pieces.append(block_of(messages, d, slice(count, count + take), slice(k * ranks, (k + 1) * ranks)))
        basis = jnp.concatenate(pieces, 0)
        out_ref[source(at_ref[0], d), :rows, :] = jnp.dot(basis, direction, preferred_element_type=f32).astype(bf16)
    parts = jnp.concatenate(three_parts(gradient_ref[...]), 0).astype(bf16)
    shape = (Y * 16, parts.shape[0])
    row, column = lax.broadcasted_iota(jnp.int32, shape, 0), lax.broadcasted_iota(jnp.int32, shape, 1)
    place = row % 16
    wanted = place // 4 * gradient_ref.shape[0] + row // 16 * 4 + place % 4
    pick = ((column == wanted) & (place < 12)).astype(bf16)
    picked = jnp.dot(pick, parts, preferred_element_type=f32).astype(bf16)
    for y in range(Y):
        out_ref[y, rows:, :] = picked[16 * y : 16 * (y + 1), :]


def finish_kernel(at_ref, arrived_ref, first_ref, second_ref, new_first_ref, new_second_ref, update_ref):
    rows = update_ref.shape[0]
    part = arrived_ref.shape[2]
    for y in range(Y):
        columns = slice(y * part, (y + 1) * part)
        update_ref[:, columns] = arrived_ref[y, :rows, :].astype(f32)
        parts = arrived_ref[y, rows:, :].astype(f32)
        gradient = parts[0:4] + parts[4:8] + parts[8:12]
        new_first, new_second = adam(first_ref[:, columns], second_ref[:, columns], gradient)
        new_first_ref[:, columns] = new_first
        new_second_ref[:, columns] = new_second


def on_device(tokens, basis, grad_out, first_moment, second_moment):
    rows, ranks = basis.shape
    count, features = tokens.shape
    share, columns = first_moment.shape
    part = columns // Y
    half = ranks // C
    core = lax.axis_index("c")
    at = jnp.stack([lax.axis_index("y"), core, lax.axis_index("l")])

    ordered_half = jnp.dot(basis, rank_order(core * half, half, ranks), preferred_element_type=f32).astype(bf16)
    turned = lax.ppermute(ordered_half, ("y", "x"), TURN)
    own_basis = gather(turned, "h", H)
    got_basis = lax.ppermute(own_basis, "l", [(0, 1), (1, 0)])

    ordered = jnp.dot(basis, rank_order(0, ranks, ranks), preferred_element_type=f32).astype(bf16)
    moments = jnp.concatenate([first_moment, second_moment], 0)
    message = (count + PACK + MOMENT_ROWS, part)
    anywhere = pl.BlockSpec(memory_space=pl.ANY)
    messages = pl.pallas_call(
        pack_kernel,
        out_shape=[jax.ShapeDtypeStruct(message, bf16)] * Y,
        in_specs=[SMEM, VMEM, VMEM, anywhere],
        out_specs=[anywhere] * Y,
        scratch_shapes=[pltpu.VMEM((Y, PACK + MOMENT_ROWS, part), bf16), pltpu.SemaphoreType.DMA((2 * Y,))],
        compiler_params=pltpu.CompilerParams(vmem_limit_bytes=32 * 2**20),
        name="pack",
    )(at, ordered, moments, grad_out)
    sent = {2: send(messages[2], 2), 1: send(messages[1], 1), 3: send_one_core(messages[3], 3, 0)}
    late = messages[3]

    tokens, first_message = lax.optimization_barrier((tokens, messages[0]))
    other = lax.ppermute(tokens, "c", [(0, 1), (1, 0)])

    (summands,) = call(project_kernel, "project", [((X, count, half), f32)], at, tokens, other, own_basis, got_basis)
    summands, sent[2] = lax.optimization_barrier((summands, sent[2]))
    summands = exchange(summands, "x")
    (projected,) = call(round_kernel, "round", [((C * Y, count, half), bf16)], at, summands)
    projected, sent[1], sent[3] = lax.optimization_barrier((projected, sent[1], sent[3]))
    messages = [first_message, sent[1], sent[2], sent[3]]
    projected = exchange(projected, ("c", "y")).reshape(C, Y, count, half)
    projected, late = lax.optimization_barrier((projected, late))
    messages = messages + [send_one_core(late, 3, 1)]


    (early,) = call(early_kernel, "early", [((ranks, part), f32)], at, projected, *messages[:Y])
    (partial,) = call(late_kernel, "partial", [((ranks, part), bf16)], at, early, projected, messages[Y])
    pieces = exchange(partial.reshape(Z, ranks // Z, part), ("h", "l"))
    gradient, direction = call(
        adam_kernel,
        "sum_and_adam",
        [((ranks // Z, part), f32), ((ranks // Z, part), bf16)],
        at,
        pieces,
        *messages,
    )
    direction = lax.all_gather(direction, ("h", "l"), axis=0, tiled=True)
    (update,) = call(update_kernel, "update", [((Y, rows + 16, part), bf16)], at, direction, gradient, *messages)
    arrived = exchange(update, "y")
    return tuple(
        call(
            finish_kernel,
            "finish",
            [((share, columns), f32), ((share, columns), f32), ((rows, columns), f32)],
            at,
            arrived,
            first_moment,
            second_moment,
        )
    )


def solution(mesh):
    grid = Mesh(mesh.devices.reshape(Y, H, L, X, C), ("y", "h", "l", "x", "c"))
    dp, col = ("y", "h", "l"), ("x", "c")
    return jax.shard_map(
        on_device,
        mesh=grid,
        in_specs=(P(dp, col), P(dp, None), P(dp, col), P(dp, col), P(dp, col)),
        out_specs=(P(dp, col), P(dp, col), P(dp, col)),
        check_vma=False,
    )
```
